128 devices in a mesh: dp: 64 (over z_hi, y, x, core), chip: 2 (over z_lo).
Axes of the slice: x: 4, y: 4, z: 4 (z_hi: 2, z_lo: 2; z = z_hi * 2 + z_lo), core: 2. Of those that a mesh axis runs over, the one named last changes fastest.
Arguments:
- moe_in: bfloat16 [2048, 3584], P(('dp', 'chip')), may hold values from -6 to 6
- expert_ids: int32 [2048, 8], P(('dp', 'chip')), may hold values from 0 to 127, as said below
- expert_gates: float32 [2048, 8], P(('dp', 'chip')), may hold values from 0.1 to 1
- gate_weight: bfloat16 [128, 3584, 1024], P(('dp', 'chip')), may hold values from -0.09375 to 0.09375
- up_weight: bfloat16 [128, 3584, 1024], P(('dp', 'chip')), may hold values from -0.09375 to 0.09375
- down_weight: bfloat16 [128, 1024, 3584], P(('dp', 'chip')), may hold values from -0.1875 to 0.1875
- queries: bfloat16 [384, 128, 576], P(('dp', 'chip')), may hold values from -14 to 14
- cache_pool: bfloat16 [3328, 64, 576], P(('dp', 'chip')), may hold values from -4 to 4
- req_source: int32 [384], replicated, may hold values from 0 to 127, as said below
- req_first: int32 [384], replicated, may hold values from 0 to 14, as said below
- req_tokens: int32 [384], replicated, may hold values from 1 to 768, as said below
Outputs:
- moe_out: bfloat16 [2048, 3584], P(('dp', 'chip'))
- attn_latent: bfloat16 [384, 128, 512], P(('dp', 'chip'))
The draws below stay inside these ranges and needn't reach their ends.
Inputs may be any that keep to these rules, and one draw needn't show every extreme that they name: `expert_ids`: expert e belongs to rank e. Each row names 8 different experts; the rows of one rank name any one expert at most 2 times; in every draw one expert is named exactly 2 times by the rows of every rank. `req_source`: request r is served by rank r // 3. Its source is that rank or one of the 1 ranks before it, cyclically; a rank serves exactly 1 request whose source lies k ranks before it, for each k from 1 to 1. `req_first`: A request's blocks lie contiguously in its source rank's 26 blocks. A rank's blocks for the requests it serves itself fill exactly its first 14 blocks; those for the request served k ranks after it fill exactly blocks 26 - (2 - k) * 12 up to 26 - (1 - k) * 12, so the request served 1 ranks after its source starts at block 14. `req_tokens`: A request has ceil(length / 64) blocks, at most 12; every rank serves a request of 768 tokens.
All inputs are finite; a program needn't handle non-finite values.
Results may differ from the reference program's by a relative error of at most 0.0058.
Values may be sent and summed in bfloat16 or wider, within the bound.
No kernel may reach another device: no remote copies, remote signals or barrier semaphores. Data moves between devices by JAX's collectives and lax.ppermute only.
A program may use at most 128 MiB of HBM per device.

```python
import math
import jax
import jax.numpy as jnp
from jax import lax

D = 3584
FF = 1024
TOP = 8
HEADS = 128
LATENT = 512
CACHE_DIM = 576
BLOCK_ROWS = 64
MAX_BLOCKS = 12
REQ_DEV = 3
HOPS = 1
MOVE_REQ = 1
MOVE_BLOCKS = 12
POOL_DEV = 26
TOK_DEV = 16
EXPERTS = 128
CAP = 2
TOKENS = 2048
REQUESTS = 384
POOL = 3328
N_DP = 64
N_CHIP = 2


def compose(seed_key, amount, pieces):
    if pieces == 1:
        return jnp.full((1,), amount, jnp.int32)
    cut_points = jnp.sort(jax.random.permutation(seed_key, amount - 1)[:pieces - 1] + 1).astype(jnp.int32)
    boundary = jnp.concatenate([jnp.zeros((1,), jnp.int32), cut_points, jnp.full((1,), amount, jnp.int32)])
    return jnp.diff(boundary)


def plan_tables(seed_key):
    seed_key = jax.random.fold_in(seed_key, 101)
    rank_total = REQUESTS // REQ_DEV
    resident = REQ_DEV - HOPS * MOVE_REQ
    hop_base = jnp.concatenate([jnp.zeros((resident,), jnp.int32), jnp.repeat(jnp.arange(1, HOPS + 1, dtype=jnp.int32), MOVE_REQ)])

    def one_rank(rank_key, rank_index):
        subkeys = jax.random.split(rank_key, 4 + HOPS)
        hop_of = jax.random.permutation(subkeys[0], hop_base)
        rest_counts = compose(subkeys[1], POOL_DEV - HOPS * MOVE_BLOCKS - MAX_BLOCKS, resident - 1)
        stacked = jnp.concatenate([jnp.full((1,), MAX_BLOCKS, jnp.int32), rest_counts])
        ordinal = jax.random.permutation(subkeys[2], resident)
        counts = jnp.zeros((REQ_DEV,), jnp.int32)
        firsts = jnp.zeros((REQ_DEV,), jnp.int32)
        longest = jnp.zeros((REQ_DEV,), bool)
        for distance in range(HOPS + 1):
            matches = hop_of == distance
            position = jnp.cumsum(matches.astype(jnp.int32)) - 1
            if distance == 0:
                group_counts = stacked[ordinal]
                group_starts = jnp.cumsum(group_counts) - group_counts
                group_long = ordinal == 0
            else:
                group_counts = compose(subkeys[3 + distance], MOVE_BLOCKS, MOVE_REQ)
                group_starts = POOL_DEV - (HOPS + 1 - distance) * MOVE_BLOCKS + jnp.cumsum(group_counts) - group_counts
                group_long = jnp.zeros((MOVE_REQ,), bool)
            clipped = jnp.clip(position, 0, group_counts.shape[0] - 1)
            counts = jnp.where(matches, group_counts[clipped], counts)
            firsts = jnp.where(matches, group_starts[clipped], firsts)
            longest = jnp.where(matches, group_long[clipped], longest)
        tail_rows = jax.random.randint(subkeys[3], (REQ_DEV,), 1, BLOCK_ROWS + 1)
        tail_rows = jnp.where(longest, BLOCK_ROWS, tail_rows)
        tokens = (counts - 1) * BLOCK_ROWS + tail_rows
        sources = jnp.mod(rank_index - hop_of, rank_total)
        return (sources.astype(jnp.int32), firsts.astype(jnp.int32), tokens.astype(jnp.int32))
    rank_keys = jax.random.split(seed_key, rank_total)
    sources, firsts, tokens = jax.vmap(one_rank)(rank_keys, jnp.arange(rank_total, dtype=jnp.int32))
    return (sources.reshape(-1), firsts.reshape(-1), tokens.reshape(-1))


def cache_normal(seed_key):
    return jax.random.normal(jax.random.fold_in(seed_key, 202), (POOL, BLOCK_ROWS, CACHE_DIM), jnp.float32)


def draw_req_source(key, part):
    return plan_tables(key)[0]


def draw_req_first(key, part):
    return plan_tables(key)[1]


def draw_req_tokens(key, part):
    return plan_tables(key)[2]


def draw_cache_pool(key, part):
    draws_raw = cache_normal(key)
    return jnp.clip(draws_raw, -4.0, 4.0).astype(jnp.bfloat16)


def draw_queries(key, part):
    own_key = jax.random.fold_in(key, 12)
    draws_raw = jax.random.normal(own_key, (REQUESTS, HEADS, CACHE_DIM), jnp.float32)
    return jnp.clip(draws_raw, -4.0, 4.0).astype(jnp.bfloat16)


def draw_expert_ids(key, part):
    seed_key = jax.random.fold_in(key, 7)
    rank_total = TOKENS // TOK_DEV
    busiest = jax.random.randint(jax.random.fold_in(seed_key, 1), (), 0, EXPERTS)

    def one_rank(rank_key):
        subkeys = jax.random.split(rank_key, 2)
        shuffled = jax.random.permutation(subkeys[0], EXPERTS).astype(jnp.int32)
        hot_place = jnp.argmax(shuffled == busiest)
        shuffled = shuffled.at[hot_place].set(shuffled[0]).at[0].set(busiest)
        gap_sizes = jax.random.randint(subkeys[1], (EXPERTS,), CAP // 2, CAP + 1).at[0].set(CAP)
        bounds = jnp.cumsum(gap_sizes)
        slot_ids = jnp.arange(TOK_DEV * TOP)
        group_of = jnp.sum((bounds[None, :] <= slot_ids[:, None]).astype(jnp.int32), axis=1)
        return shuffled[group_of].reshape(TOP, TOK_DEV).T
    rank_keys = jax.random.split(jax.random.fold_in(seed_key, 2), rank_total)
    return jax.vmap(one_rank)(rank_keys).reshape(TOKENS, TOP).astype(jnp.int32)


def block_scale(key, dims, cuts, least, largest):
    loudness = 1.0
    for axis_at, shards_of in cuts:
        draws = jax.random.uniform(jax.random.fold_in(jax.random.fold_in(key, 6), axis_at), (shards_of,), jnp.float32, least / len(cuts), largest / len(cuts))
        loudness = loudness * jnp.repeat(jnp.exp(draws), dims[axis_at] // shards_of).reshape((-1,) + (1,) * (len(dims) - 1 - axis_at))
    return loudness


def centred(key, shape, scale, most, shards=(), kind=jnp.bfloat16):
    drawn = jax.random.normal(key, shape, jnp.float32) * scale
    if len(shards) > 0:
        drawn = block_scale(key, shape, shards, -0.22, 0.18) * drawn
    return jnp.clip(drawn, min=-most, max=most).astype(kind)


def setup_inputs(seed: int = 0) -> dict:
    key_of = jax.random.split(jax.random.key(seed), 12)
    moe_in = centred(key_of[0], (TOKENS, D), 1.0, 6.0, ((0, 128),))
    expert_ids = draw_expert_ids(jax.random.fold_in(key_of[11], 71), 0)
    expert_gates = jnp.clip(jnp.exp(math.log(1.0) - 2.3025851 * jax.random.uniform(key_of[2], (TOKENS, TOP), jnp.float32) ** block_scale(key_of[2], (TOKENS, TOP), ((0, 128),), -0.2, 0.2)), 0.1, 1.0)
    gate_weight = centred(key_of[3], (EXPERTS, D, FF), D ** -0.5, 0.09375, ((0, 128),))
    up_weight = centred(key_of[4], (EXPERTS, D, FF), D ** -0.5, 0.09375, ((0, 128),))
    down_weight = centred(key_of[5], (EXPERTS, FF, D), FF ** -0.5, 0.1875, ((0, 128),))
    queries = draw_queries(jax.random.fold_in(key_of[11], 71), 0)
    cache_pool = draw_cache_pool(jax.random.fold_in(key_of[11], 71), 0)
    req_source = draw_req_source(jax.random.fold_in(key_of[11], 71), 0)
    req_first = draw_req_first(jax.random.fold_in(key_of[11], 71), 0)
    req_tokens = draw_req_tokens(jax.random.fold_in(key_of[11], 71), 0)
    return {"moe_in": moe_in, "expert_ids": expert_ids, "expert_gates": expert_gates, "gate_weight": gate_weight, "up_weight": up_weight, "down_weight": down_weight, "queries": queries, "cache_pool": cache_pool, "req_source": req_source, "req_first": req_first, "req_tokens": req_tokens}


score_scale = 1.0 / math.sqrt(192.0)

def attend(query_rows, cache_rows, lengths):
    scores = jnp.einsum('rhd,rtd->rht', query_rows.astype(jnp.float32), cache_rows.astype(jnp.float32)) * score_scale
    in_range = jnp.arange(cache_rows.shape[1])[None, None, :] < lengths[:, None, None]
    row_max = lax.optimization_barrier(jnp.max(jnp.where(in_range, scores, -1e+30), axis=-1, keepdims=True))
    weights = jnp.where(in_range, jnp.exp(scores - row_max), 0.0)
    softmax_out = (weights / lax.optimization_barrier(jnp.sum(weights, axis=-1, keepdims=True))).astype(jnp.bfloat16)
    latent_rows = cache_rows[:, :, :LATENT]
    return jnp.einsum('rht,rtc->rhc', softmax_out.astype(jnp.float32), latent_rows.astype(jnp.float32)).astype(jnp.bfloat16)

def moe_block(moe_in, expert_ids, expert_gates, gate_weight, up_weight, down_weight):
    flat_ids = expert_ids.reshape(-1)
    flat_gates = expert_gates.reshape(-1)
    row_of = (jnp.arange(flat_ids.shape[0]) // TOP).astype(jnp.int32)

    def one_expert(totals, expert):
        matches = flat_ids == expert
        slot_ids = jnp.nonzero(matches, size=N_DP * N_CHIP * CAP, fill_value=0)[0].astype(jnp.int32)
        filled = jnp.arange(slot_ids.shape[0]) < jnp.sum(matches.astype(jnp.int32))
        picked_rows = moe_in[row_of[slot_ids]]
        gate_part = jnp.dot(picked_rows, gate_weight[expert], preferred_element_type=jnp.float32)
        up_part = jnp.dot(picked_rows, up_weight[expert], preferred_element_type=jnp.float32)
        hidden = (jax.nn.silu(gate_part) * up_part).astype(jnp.bfloat16)
        answered = jnp.dot(hidden, down_weight[expert], preferred_element_type=jnp.float32).astype(jnp.bfloat16)
        scaled = jnp.where(filled, flat_gates[slot_ids], 0.0)[:, None] * answered.astype(jnp.float32)
        return (totals.at[row_of[slot_ids]].add(scaled), None)
    totals = lax.scan(one_expert, jnp.zeros((TOKENS, D), jnp.float32), jnp.arange(EXPERTS, dtype=jnp.int32))[0]
    return totals.astype(jnp.bfloat16)

def latent_attention(queries, cache_pool, req_source, req_first, req_tokens):

    def one_rank(rank_index):
        first_slot = rank_index * REQ_DEV
        sources = lax.dynamic_slice_in_dim(req_source, first_slot, REQ_DEV)
        firsts = lax.dynamic_slice_in_dim(req_first, first_slot, REQ_DEV)
        lengths = lax.dynamic_slice_in_dim(req_tokens, first_slot, REQ_DEV)
        query_rows = lax.dynamic_slice_in_dim(queries, first_slot, REQ_DEV)
        block_index = sources[:, None] * POOL_DEV + firsts[:, None] + jnp.arange(MAX_BLOCKS, dtype=jnp.int32)[None, :]
        block_index = jnp.minimum(block_index, POOL - 1).astype(jnp.int32)
        cache_rows = cache_pool[block_index.reshape(-1)].reshape(REQ_DEV, MAX_BLOCKS * BLOCK_ROWS, CACHE_DIM)
        return attend(query_rows, cache_rows, lengths)
    outputs = lax.map(one_rank, jnp.arange(N_DP * N_CHIP, dtype=jnp.int32))
    return outputs.reshape(REQUESTS, HEADS, LATENT)

def reference(moe_in, expert_ids, expert_gates, gate_weight, up_weight, down_weight, queries, cache_pool, req_source, req_first, req_tokens):
    moe_out = moe_block(moe_in, expert_ids, expert_gates, gate_weight, up_weight, down_weight)
    attn_latent = latent_attention(queries, cache_pool, req_source, req_first, req_tokens)
    return (moe_out, attn_latent)
```

```python
import math

import jax
import jax.numpy as jnp
from jax import lax
from jax.experimental import pallas as pl
from jax.experimental.pallas import tpu as pltpu
from jax.sharding import PartitionSpec as P

LATENT = 512
MAX_BLOCKS = 12
POOL = 26
REQUESTS = 3
SLOTS = 2
PARTS = 4
LANES = 128
MIB = 1 << 20
STEP = 256

score_scale = 1.0 / math.sqrt(192.0)

VMEM = pl.BlockSpec(memory_space=pltpu.VMEM)
SMEM = pl.BlockSpec(memory_space=pltpu.SMEM)
HBM = pl.BlockSpec(memory_space=pltpu.HBM)
AXES = ("dp", "chip")


def call(kernel, out_shape, in_specs, out_specs, scratch=(), limit=24 * MIB, aliases={}):
    return pl.pallas_call(
        kernel,
        out_shape=out_shape,
        in_specs=in_specs,
        out_specs=out_specs,
        scratch_shapes=scratch,
        input_output_aliases=aliases,
        compiler_params=pltpu.CompilerParams(vmem_limit_bytes=limit),
    )


def dot(a, b, contract=((1,), (0,))):
    return lax.dot_general(a, b, (contract, ((), ())), preferred_element_type=jnp.float32)


def moved_at(source_ref, rank, per_rank):
    first = rank * per_rank
    at = jnp.int32(0)
    for i in range(1, per_rank):
        at = jnp.where(source_ref[first + i] != rank, i, at)
    return at


def iota(shape, dim):
    return lax.broadcasted_iota(jnp.int32, shape, dim)


def send_kernel(source_hbm, ids_hbm, x_hbm, queries_hbm, out_hbm, query_ref, source_ref, ids_ref, x_ref, queries_ref, out_ref, sems):
    pairs = ((ids_hbm, ids_ref), (x_hbm, x_ref), (source_hbm, source_ref), (queries_hbm, queries_ref))
    fetches = [pltpu.make_async_copy(here, there, sems.at[i]) for i, (here, there) in enumerate(pairs)]
    for fetch in fetches:
        fetch.start()
    top, rows = ids_ref.shape
    messages, piece = out_ref.shape
    place_count = SLOTS * PARTS
    ranks = messages // place_count
    columns = PARTS * rows
    shape = (columns, columns)
    before = (iota(shape, 0) // rows == iota(shape, 1) // rows) & (iota(shape, 0) < iota(shape, 1))
    before = before.astype(jnp.bfloat16)
    expert = iota((ranks, columns), 0)
    fetches[0].wait()
    ids = jnp.concatenate([ids_ref[...]] * PARTS, axis=1)
    named = jnp.zeros((ranks, columns), jnp.float32)
    for k in range(top):
        named += (ids[k : k + 1, :] == expert).astype(jnp.float32)
    named = named.astype(jnp.bfloat16)
    slot = jnp.where(named > 0, dot(named, before), -1.0).astype(jnp.bfloat16)
    fetches[1].wait()
    pieces = jnp.concatenate([x_ref[:, p * piece : (p + 1) * piece] for p in range(PARTS)], axis=0)
    steps = 4
    step = messages // steps
    sends = []
    for n in range(steps):
        at = n * step
        spread = ((iota((step, ranks), 0) + at) // place_count == iota((step, ranks), 1)).astype(jnp.bfloat16)
        place = iota((step, columns), 0) % place_count
        hit = (dot(spread, slot) == (place // PARTS).astype(jnp.float32)) & (place % PARTS == iota((step, columns), 1) // rows)
        out_ref[at : at + step, :] = dot(hit.astype(jnp.bfloat16), pieces).astype(jnp.bfloat16)
        sends.append(pltpu.make_async_copy(out_ref.at[pl.ds(at, step)], out_hbm.at[pl.ds(at, step)], sems.at[4 + n]))
        sends[-1].start()
    fetches[2].wait()
    fetches[3].wait()
    query_ref[...] = queries_ref[moved_at(source_ref, lax.axis_index(AXES), REQUESTS)]
    for send in sends:
        send.wait()


def attend(query_cols, cache_rows, length):
    scores = dot(cache_rows, query_cols) * score_scale
    in_range = iota(scores.shape, 0) < length
    row_max = jnp.max(jnp.where(in_range, scores, -1e30), axis=0, keepdims=True)
    weights = jnp.where(in_range, jnp.exp(scores - row_max), 0.0)
    softmax_out = (weights / jnp.sum(weights, axis=0, keepdims=True)).astype(jnp.bfloat16)
    return dot(softmax_out, cache_rows[:, :LATENT], ((0,), (0,))).astype(jnp.bfloat16)


def spread_gates(ids_ref, gates_ref, out_ref):
    rows, top = ids_ref.shape
    messages = out_ref.shape[1]
    place_count = SLOTS * PARTS
    ranks = messages // place_count
    expert = iota((rows, ranks), 1)
    named = jnp.zeros((rows, ranks), jnp.float32)
    rest = jnp.zeros((rows, ranks), jnp.float32)
    for k in range(top):
        chosen = ids_ref[:, k : k + 1] == expert
        named += chosen.astype(jnp.float32)
        rest += jnp.where(chosen, gates_ref[:, k : k + 1], 0.0)
    before = (iota((rows, rows), 1) < iota((rows, rows), 0)).astype(jnp.bfloat16)
    slot = jnp.where(named > 0, dot(before, named.astype(jnp.bfloat16)), -1.0)
    shape = (ranks, messages)
    spread = (iota(shape, 1) // place_count == iota(shape, 0)).astype(jnp.bfloat16)
    place = iota((rows, messages), 1) % place_count
    hit = dot(slot.astype(jnp.bfloat16), spread) == (place // PARTS).astype(jnp.float32)
    for third in range(3):
        head = rest.astype(jnp.bfloat16)
        rest = rest - head.astype(jnp.float32)
        spread_head = jnp.where(hit, dot(head, spread), 0.0)
        for p in range(PARTS):
            at = (third * PARTS + p) * rows
            out_ref[at : at + rows, :] = jnp.where(place % PARTS == p, spread_head, 0.0).astype(jnp.bfloat16)


def window(cache_ref, first):
    block_rows = cache_ref.shape[0] // POOL
    start = pl.multiple_of(first * block_rows, block_rows)
    return cache_ref[pl.ds(start, MAX_BLOCKS * block_rows), :]


def own_kernel(source_ref, first_ref, tokens_ref, queries_ref, cache_ref, ids_ref, gates_ref, attn_ref, spread_ref):
    spread_gates(ids_ref, gates_ref, spread_ref)
    my_rank = lax.axis_index(AXES)
    mine = moved_at(source_ref, my_rank, REQUESTS)
    for r in (jnp.where(mine == 0, 1, 0), jnp.where(mine == 2, 1, 2)):
        n = my_rank * REQUESTS + r
        attn_ref[r] = attend(queries_ref[r], window(cache_ref, first_ref[n]), tokens_ref[n])
    attn_ref[mine] = jnp.zeros(attn_ref.shape[1:], attn_ref.dtype)


def moved_kernel(source_ref, first_ref, tokens_ref, query_ref, cache_ref, out_ref):
    next_rank = lax.rem(lax.axis_index(AXES) + 1, source_ref.shape[0] // REQUESTS)
    n = next_rank * REQUESTS + moved_at(source_ref, next_rank, REQUESTS)
    out_ref[...] = attend(query_ref[...], window(cache_ref, first_ref[n]), tokens_ref[n])


def expert_kernel(x_ref, gate_hbm, up_hbm, down_hbm, out_ref, gate_ref, up_ref, down_ref, wide, flat, hidden, sems):
    messages, piece = x_ref.shape
    units = hidden.shape[1]
    place_count = SLOTS * PARTS
    ranks = messages // place_count
    strips = piece // LANES
    count = 0

    def fetch(here, there, at, width):
        nonlocal count
        columns = pl.ds(at, width)
        copy = pltpu.make_async_copy(here.at[:, columns], there.at[:, columns], sems.at[count])
        copy.start()
        count += 1
        return copy

    near = [(fetch(gate_hbm, gate_ref, n, STEP), fetch(up_hbm, up_ref, n, STEP)) for n in range(0, units, STEP)]
    lows = range(0, piece, STEP)
    far = [[fetch(down_hbm, down_ref, p * piece + low, min(STEP, piece - low)) for p in range(PARTS)] for low in lows]
    for c in range(strips):
        wide[c] = x_ref[:, c * LANES : (c + 1) * LANES].astype(jnp.float32)
    for place in range(place_count):
        s, p = divmod(place, PARTS)
        for c in range(strips):
            at = p * piece + c * LANES
            taken = wide[c, pl.ds(place, ranks, stride=place_count), :]
            flat[s * ranks : (s + 1) * ranks, at : at + LANES] = taken.astype(jnp.bfloat16)
    for n, group in zip(range(0, units, STEP), near):
        for copy in group:
            copy.wait()
        gate_part = dot(flat[...], gate_ref[:, n : n + STEP])
        up_part = dot(flat[...], up_ref[:, n : n + STEP])
        hidden[:, n : n + STEP] = (gate_part / (1.0 + jnp.exp(-gate_part)) * up_part).astype(jnp.bfloat16)
    for low, group in zip(lows, far):
        high = min(low + STEP, piece)
        for copy in group:
            copy.wait()
        for p in range(PARTS):
            result = dot(hidden[...], down_ref[:, p * piece + low : p * piece + high])
            for s in range(SLOTS):
                for c in range(low // LANES, high // LANES):
                    at = c * LANES - low
                    kept = result[s * ranks : (s + 1) * ranks, at : at + LANES]
                    wide[c, pl.ds(s * PARTS + p, ranks, stride=place_count), :] = kept
        for c in range(low // LANES, high // LANES):
            out_ref[:, c * LANES : (c + 1) * LANES] = wide[c].astype(jnp.bfloat16)


def combine_kernel(source_ref, gates_ref, returned_ref, moved_hbm, attn_hbm, out_ref, attn_out_hbm, sem):
    del attn_hbm
    my_rank = lax.axis_index(AXES)
    mine = moved_at(source_ref, my_rank, REQUESTS)
    copy = pltpu.make_async_copy(moved_hbm, attn_out_hbm.at[mine], sem)
    copy.start()
    rows = out_ref.shape[0]
    piece = returned_ref.shape[1]
    total = dot(gates_ref[...], returned_ref[...])
    for p in range(PARTS):
        thirds = [total[(third * PARTS + p) * rows : (third * PARTS + p + 1) * rows] for third in range(3)]
        out_ref[:, p * piece : (p + 1) * piece] = (thirds[0] + thirds[1] + thirds[2]).astype(jnp.bfloat16)
    copy.wait()


def per_device(
    moe_in,
    expert_ids,
    expert_gates,
    gate_weight,
    up_weight,
    down_weight,
    queries,
    cache_pool,
    req_source,
    req_first,
    req_tokens,
):
    group_size = lax.axis_size(AXES)
    row_count, model_width = moe_in.shape
    place_count = SLOTS * PARTS
    messages = group_size * place_count
    piece = model_width // PARTS
    units = gate_weight.shape[2]
    heads, features = queries.shape[1:]
    bf16 = jnp.bfloat16
    dma = pltpu.SemaphoreType.DMA

    def exchange(x):
        x = x.reshape(group_size, place_count, piece)
        return lax.all_to_all(x, AXES, split_axis=0, concat_axis=0, tiled=True).reshape(messages, piece)

    def to_rank(x, distance):
        return lax.ppermute(x, AXES, [(i, (i + distance) % group_size) for i in range(group_size)])

    def stay(*arrays):
        return [pltpu.with_memory_space_constraint(x, pltpu.HBM) for x in arrays]

    message = (messages, piece)
    query_cols = jnp.swapaxes(queries, 1, 2)
    outgoing, moved_query = call(
        send_kernel,
        (pltpu.HBM(message, bf16), jax.ShapeDtypeStruct((features, heads), bf16)),
        [HBM] * 4,
        (HBM, VMEM),
        [
            pltpu.SMEM(req_source.shape, jnp.int32),
            pltpu.VMEM(expert_ids.shape[::-1], jnp.int32),
            pltpu.VMEM(moe_in.shape, bf16),
            pltpu.VMEM(query_cols.shape, bf16),
            pltpu.VMEM(message, bf16),
            dma((8,)),
        ],
    )(*stay(req_source, expert_ids.T, moe_in, query_cols))
    moved_query = to_rank(moved_query, -1)
    arrived = exchange(outgoing)

    cache_rows = cache_pool.reshape(-1, features)
    plan = (req_source, req_first, req_tokens)
    attn_own, gates = call(
        own_kernel,
        (
            jax.ShapeDtypeStruct((REQUESTS, heads, LATENT), bf16),
            jax.ShapeDtypeStruct((3 * PARTS * row_count, messages), bf16),
        ),
        [SMEM] * 3 + [VMEM] * 4,
        (VMEM,) * 2,
    )(*plan, query_cols, cache_rows, expert_ids, expert_gates)
    moved_out = call(moved_kernel, jax.ShapeDtypeStruct((heads, LATENT), bf16), [SMEM] * 3 + [VMEM] * 2, VMEM)(
        *plan, moved_query, cache_rows
    )
    arrived, moved_out, attn_own, gates = lax.optimization_barrier((arrived, moved_out, attn_own, gates))
    moved_out = to_rank(moved_out, 1)
    answered = call(
        expert_kernel,
        jax.ShapeDtypeStruct(message, bf16),
        [VMEM] + [HBM] * 3,
        VMEM,
        [
            pltpu.VMEM(gate_weight.shape[1:], bf16),
            pltpu.VMEM(up_weight.shape[1:], bf16),
            pltpu.VMEM(down_weight.shape[1:], bf16),
            pltpu.VMEM((piece // LANES, messages, LANES), jnp.float32),
            pltpu.VMEM((SLOTS * group_size, model_width), bf16),
            pltpu.VMEM((SLOTS * group_size, units), bf16),
            dma((2 * (units // STEP) + PARTS * -(-piece // STEP),)),
        ],
        limit=44 * MIB,
    )(arrived, *stay(gate_weight[0], up_weight[0], down_weight[0]))
    answered, moved_out = lax.optimization_barrier((answered, moved_out))
    returned = exchange(answered)
    moe_out, attn_latent = call(
        combine_kernel,
        (jax.ShapeDtypeStruct(moe_in.shape, bf16), jax.ShapeDtypeStruct(attn_own.shape, bf16)),
        [SMEM, VMEM, VMEM, HBM, HBM],
        (VMEM, HBM),
        [dma],
        aliases={4: 1},
    )(req_source, gates, returned, moved_out, attn_own)
    return (moe_out, attn_latent)


def solution(mesh):
    rows = P(("dp", "chip"), None)
    blocks = P(("dp", "chip"), None, None)
    return jax.shard_map(
        per_device,
        mesh=mesh,
        in_specs=(rows, rows, rows, blocks, blocks, blocks, blocks, blocks, P(), P(), P()),
        out_specs=(rows, blocks),
        check_vma=False,
    )
```

```python
import math

import jax
import jax.numpy as jnp
from jax import lax
from jax.experimental import pallas as pl
from jax.experimental.pallas import tpu as pltpu
from jax.sharding import PartitionSpec as P

LATENT = 512
MAX_BLOCKS = 12
POOL = 26
REQUESTS = 3
SLOTS = 2
PARTS = 4
LANES = 128
MIB = 1 << 20
STEP = 256

score_scale = 1.0 / math.sqrt(192.0)

VMEM = pl.BlockSpec(memory_space=pltpu.VMEM)
SMEM = pl.BlockSpec(memory_space=pltpu.SMEM)
HBM = pl.BlockSpec(memory_space=pltpu.HBM)
AXES = ("dp", "chip")


def call(kernel, out_shape, in_specs, out_specs, scratch=(), limit=24 * MIB, aliases={}):
    return pl.pallas_call(
        kernel,
        out_shape=out_shape,
        in_specs=in_specs,
        out_specs=out_specs,
        scratch_shapes=scratch,
        input_output_aliases=aliases,
        compiler_params=pltpu.CompilerParams(vmem_limit_bytes=limit),
    )


def dot(a, b, contract=((1,), (0,))):
    return lax.dot_general(a, b, (contract, ((), ())), preferred_element_type=jnp.float32)


def moved_at(source_ref, rank, per_rank):
    first = rank * per_rank
    at = jnp.int32(0)
    for i in range(1, per_rank):
        at = jnp.where(source_ref[first + i] != rank, i, at)
    return at


def iota(shape, dim):
    return lax.broadcasted_iota(jnp.int32, shape, dim)


def send_kernel(source_hbm, ids_hbm, x_hbm, queries_hbm, out_hbm, query_ref, source_ref, ids_ref, x_ref, queries_ref, out_ref, sems):
    pairs = ((ids_hbm, ids_ref), (x_hbm, x_ref), (source_hbm, source_ref), (queries_hbm, queries_ref))
    fetches = [pltpu.make_async_copy(here, there, sems.at[i]) for i, (here, there) in enumerate(pairs)]
    for fetch in fetches:
        fetch.start()
    top, rows = ids_ref.shape
    messages, piece = out_ref.shape
    place_count = SLOTS * PARTS
    ranks = messages // place_count
    columns = PARTS * rows
    shape = (columns, columns)
    before = (iota(shape, 0) // rows == iota(shape, 1) // rows) & (iota(shape, 0) < iota(shape, 1))
    before = before.astype(jnp.bfloat16)
    expert = iota((ranks, columns), 0)
    fetches[0].wait()
    ids = jnp.concatenate([ids_ref[...]] * PARTS, axis=1)
    named = jnp.zeros((ranks, columns), jnp.float32)
    for k in range(top):
        named += (ids[k : k + 1, :] == expert).astype(jnp.float32)
    named = named.astype(jnp.bfloat16)
    slot = jnp.where(named > 0, dot(named, before), -1.0).astype(jnp.bfloat16)
    fetches[1].wait()
    pieces = jnp.concatenate([x_ref[:, p * piece : (p + 1) * piece] for p in range(PARTS)], axis=0)
    steps = 4
    step = messages // steps
    sends = []
    for n in range(steps):
        at = n * step
        spread = ((iota((step, ranks), 0) + at) // place_count == iota((step, ranks), 1)).astype(jnp.bfloat16)
        place = iota((step, columns), 0) % place_count
        hit = (dot(spread, slot) == (place // PARTS).astype(jnp.float32)) & (place % PARTS == iota((step, columns), 1) // rows)
        out_ref[at : at + step, :] = dot(hit.astype(jnp.bfloat16), pieces).astype(jnp.bfloat16)
        sends.append(pltpu.make_async_copy(out_ref.at[pl.ds(at, step)], out_hbm.at[pl.ds(at, step)], sems.at[4 + n]))
        sends[-1].start()
    fetches[2].wait()
    fetches[3].wait()
    query_ref[...] = queries_ref[moved_at(source_ref, lax.axis_index(AXES), REQUESTS)]
    for send in sends:
        send.wait()


def attend(query_cols, cache_rows, length):
    scores = dot(cache_rows, query_cols) * score_scale
    in_range = iota(scores.shape, 0) < length
    row_max = jnp.max(jnp.where(in_range, scores, -1e30), axis=0, keepdims=True)
    weights = jnp.where(in_range, jnp.exp(scores - row_max), 0.0)
    softmax_out = (weights / jnp.sum(weights, axis=0, keepdims=True)).astype(jnp.bfloat16)
    return dot(softmax_out, cache_rows[:, :LATENT], ((0,), (0,))).astype(jnp.bfloat16)


def spread_gates(ids_ref, gates_ref, out_ref):
    rows, top = ids_ref.shape
    messages = out_ref.shape[1]
    place_count = SLOTS * PARTS
    ranks = messages // place_count
    expert = iota((rows, ranks), 1)
    named = jnp.zeros((rows, ranks), jnp.float32)
    rest = jnp.zeros((rows, ranks), jnp.float32)
    for k in range(top):
        chosen = ids_ref[:, k : k + 1] == expert
        named += chosen.astype(jnp.float32)
        rest += jnp.where(chosen, gates_ref[:, k : k + 1], 0.0)
    before = (iota((rows, rows), 1) < iota((rows, rows), 0)).astype(jnp.bfloat16)
    slot = jnp.where(named > 0, dot(before, named.astype(jnp.bfloat16)), -1.0)
    shape = (ranks, messages)
    spread = (iota(shape, 1) // place_count == iota(shape, 0)).astype(jnp.bfloat16)
    place = iota((rows, messages), 1) % place_count
    hit = dot(slot.astype(jnp.bfloat16), spread) == (place // PARTS).astype(jnp.float32)
    for third in range(3):
        head = rest.astype(jnp.bfloat16)
        rest = rest - head.astype(jnp.float32)
        out_ref[third * rows : (third + 1) * rows, :] = jnp.where(hit, dot(head, spread), 0.0).astype(jnp.bfloat16)


def window(cache_ref, first):
    block_rows = cache_ref.shape[0] // POOL
    start = pl.multiple_of(first * block_rows, block_rows)
    return cache_ref[pl.ds(start, MAX_BLOCKS * block_rows), :]


def own_kernel(source_ref, first_ref, tokens_ref, queries_ref, cache_ref, ids_ref, gates_ref, attn_ref, spread_ref):
    spread_gates(ids_ref, gates_ref, spread_ref)
    my_rank = lax.axis_index(AXES)
    mine = moved_at(source_ref, my_rank, REQUESTS)
    for r in (jnp.where(mine == 0, 1, 0), jnp.where(mine == 2, 1, 2)):
        n = my_rank * REQUESTS + r
        attn_ref[r] = attend(queries_ref[r], window(cache_ref, first_ref[n]), tokens_ref[n])
    attn_ref[mine] = jnp.zeros(attn_ref.shape[1:], attn_ref.dtype)


def moved_kernel(source_ref, first_ref, tokens_ref, query_ref, cache_ref, out_ref):
    next_rank = lax.rem(lax.axis_index(AXES) + 1, source_ref.shape[0] // REQUESTS)
    n = next_rank * REQUESTS + moved_at(source_ref, next_rank, REQUESTS)
    out_ref[...] = attend(query_ref[...], window(cache_ref, first_ref[n]), tokens_ref[n])


def expert_kernel(x_ref, gate_hbm, up_hbm, down_hbm, out_hbm, gate_ref, up_ref, down_ref, out_ref, wide, flat, hidden, sems):
    messages, piece = x_ref.shape
    units = hidden.shape[1]
    place_count = SLOTS * PARTS
    ranks = messages // place_count
    strips = piece // LANES
    count = 0

    def fetch(here, there, at, width):
        nonlocal count
        columns = pl.ds(at, width)
        copy = pltpu.make_async_copy(here.at[:, columns], there.at[:, columns], sems.at[count])
        copy.start()
        count += 1
        return copy

    near = [(fetch(gate_hbm, gate_ref, n, STEP), fetch(up_hbm, up_ref, n, STEP)) for n in range(0, units, STEP)]
    lows = range(0, piece, STEP)
    far = [[fetch(down_hbm, down_ref, p * piece + low, min(STEP, piece - low)) for p in range(PARTS)] for low in lows]
    for c in range(strips):
        wide[c] = x_ref[:, c * LANES : (c + 1) * LANES].astype(jnp.float32)
    for place in range(place_count):
        s, p = divmod(place, PARTS)
        for c in range(strips):
            at = p * piece + c * LANES
            taken = wide[c, pl.ds(place, ranks, stride=place_count), :]
            flat[s * ranks : (s + 1) * ranks, at : at + LANES] = taken.astype(jnp.bfloat16)
    for n, group in zip(range(0, units, STEP), near):
        for copy in group:
            copy.wait()
        gate_part = dot(flat[...], gate_ref[:, n : n + STEP])
        up_part = dot(flat[...], up_ref[:, n : n + STEP])
        hidden[:, n : n + STEP] = (gate_part / (1.0 + jnp.exp(-gate_part)) * up_part).astype(jnp.bfloat16)
    sends = []
    for low, group in zip(lows, far):
        high = min(low + STEP, piece)
        for copy in group:
            copy.wait()
        for p in range(PARTS):
            result = dot(hidden[...], down_ref[:, p * piece + low : p * piece + high])
            for s in range(SLOTS):
                for c in range(low // LANES, high // LANES):
                    at = c * LANES - low
                    kept = result[s * ranks : (s + 1) * ranks, at : at + LANES]
                    wide[c, pl.ds(s * PARTS + p, ranks, stride=place_count), :] = kept
        for c in range(low // LANES, high // LANES):
            out_ref[:, c * LANES : (c + 1) * LANES] = wide[c].astype(jnp.bfloat16)
        columns = pl.ds(low, high - low)
        sends.append(pltpu.make_async_copy(out_ref.at[:, columns], out_hbm.at[:, columns], sems.at[count + len(sends)]))
        sends[-1].start()
    for send in sends:
        send.wait()


def combine_kernel(source_hbm, gates_hbm, returned_hbm, moved_ref, attn_hbm, out_ref, attn_out_hbm, source_ref, gates_ref, returned_ref, sems):
    del attn_hbm
    messages, piece = returned_ref.shape
    steps = 4
    step = messages // steps
    gates_copy = pltpu.make_async_copy(gates_hbm, gates_ref, sems.at[0])
    source_copy = pltpu.make_async_copy(source_hbm, source_ref, sems.at[1])
    gates_copy.start()
    arrivals = []
    for n in range(steps):
        at = pl.ds(n * step, step)
        arrivals.append(pltpu.make_async_copy(returned_hbm.at[at], returned_ref.at[at], sems.at[3 + n]))
        arrivals[-1].start()
    source_copy.start()
    rows = out_ref.shape[0]
    source_copy.wait()
    mine = moved_at(source_ref, lax.axis_index(AXES), REQUESTS)
    copy = pltpu.make_async_copy(moved_ref, attn_out_hbm.at[mine], sems.at[2])
    copy.start()
    gates_copy.wait()
    part = iota((3 * rows, step), 1) % PARTS
    total = jnp.zeros((PARTS * 3 * rows, piece), jnp.float32)
    for n, arrival in enumerate(arrivals):
        at = slice(n * step, (n + 1) * step)
        gates = gates_ref[:, at]
        split = jnp.concatenate([jnp.where(part == p, gates, jnp.zeros_like(gates)) for p in range(PARTS)], axis=0)
        arrival.wait()
        total += dot(split, returned_ref[at, :])
    for p in range(PARTS):
        thirds = [total[(p * 3 + third) * rows : (p * 3 + third + 1) * rows] for third in range(3)]
        out_ref[:, p * piece : (p + 1) * piece] = (thirds[0] + thirds[1] + thirds[2]).astype(jnp.bfloat16)
    copy.wait()


def per_device(
    moe_in,
    expert_ids,
    expert_gates,
    gate_weight,
    up_weight,
    down_weight,
    queries,
    cache_pool,
    req_source,
    req_first,
    req_tokens,
):
    group_size = lax.axis_size(AXES)
    row_count, model_width = moe_in.shape
    place_count = SLOTS * PARTS
    messages = group_size * place_count
    piece = model_width // PARTS
    units = gate_weight.shape[2]
    heads, features = queries.shape[1:]
    bf16 = jnp.bfloat16
    dma = pltpu.SemaphoreType.DMA

    def exchange(x):
        x = x.reshape(group_size, place_count, piece)
        return lax.all_to_all(x, AXES, split_axis=0, concat_axis=0, tiled=True).reshape(messages, piece)

    def to_rank(x, distance):
        return lax.ppermute(x, AXES, [(i, (i + distance) % group_size) for i in range(group_size)])

    def stay(*arrays):
        return [pltpu.with_memory_space_constraint(x, pltpu.HBM) for x in arrays]

    message = (messages, piece)
    query_cols = jnp.swapaxes(queries, 1, 2)
    cache_rows = cache_pool.reshape(-1, features)
    outgoing, moved_query = call(
        send_kernel,
        (pltpu.HBM(message, bf16), jax.ShapeDtypeStruct((features, heads), bf16)),
        [HBM] * 4,
        (HBM, VMEM),
        [
            pltpu.SMEM(req_source.shape, jnp.int32),
            pltpu.VMEM(expert_ids.shape[::-1], jnp.int32),
            pltpu.VMEM(moe_in.shape, bf16),
            pltpu.VMEM(query_cols.shape, bf16),
            pltpu.VMEM(message, bf16),
            dma((8,)),
        ],
    )(*stay(req_source, expert_ids.T, moe_in, query_cols))
    moved_query = to_rank(moved_query, -1)
    arrived = exchange(outgoing)

    plan = (req_source, req_first, req_tokens)
    answered = call(
        expert_kernel,
        pltpu.HBM(message, bf16),
        [VMEM] + [HBM] * 3,
        HBM,
        [
            pltpu.VMEM(gate_weight.shape[1:], bf16),
            pltpu.VMEM(up_weight.shape[1:], bf16),
            pltpu.VMEM(down_weight.shape[1:], bf16),
            pltpu.VMEM(message, bf16),
            pltpu.VMEM((piece // LANES, messages, LANES), jnp.float32),
            pltpu.VMEM((SLOTS * group_size, model_width), bf16),
            pltpu.VMEM((SLOTS * group_size, units), bf16),
            dma((2 * (units // STEP) + (PARTS + 1) * -(-piece // STEP),)),
        ],
        limit=44 * MIB,
    )(arrived, *stay(gate_weight[0], up_weight[0], down_weight[0]))
    answered, moved_query, query_cols, cache_rows = lax.optimization_barrier((answered, moved_query, query_cols, cache_rows))
    returned = exchange(answered)
    attn_own, gates = call(
        own_kernel,
        (
            jax.ShapeDtypeStruct((REQUESTS, heads, LATENT), bf16),
            jax.ShapeDtypeStruct((3 * row_count, messages), bf16),
        ),
        [SMEM] * 3 + [VMEM] * 4,
        (VMEM,) * 2,
    )(*plan, query_cols, cache_rows, expert_ids, expert_gates)
    moved_out = call(moved_kernel, jax.ShapeDtypeStruct((heads, LATENT), bf16), [SMEM] * 3 + [VMEM] * 2, VMEM)(
        *plan, moved_query, cache_rows
    )
    moved_out = to_rank(moved_out, 1)
    moe_out, attn_latent = call(
        combine_kernel,
        (jax.ShapeDtypeStruct(moe_in.shape, bf16), pltpu.HBM(attn_own.shape, bf16)),
        [HBM] * 3 + [VMEM, HBM],
        (VMEM, HBM),
        [
            pltpu.SMEM(req_source.shape, jnp.int32),
            pltpu.VMEM(gates.shape, bf16),
            pltpu.VMEM(message, bf16),
            dma((7,)),
        ],
        aliases={4: 1},
    )(*stay(req_source, gates, returned), moved_out, *stay(attn_own))
    return (moe_out, attn_latent)


def solution(mesh):
    rows = P(("dp", "chip"), None)
    blocks = P(("dp", "chip"), None, None)
    return jax.shard_map(
        per_device,
        mesh=mesh,
        in_specs=(rows, rows, rows, blocks, blocks, blocks, blocks, blocks, P(), P(), P()),
        out_specs=(rows, blocks),
        check_vma=False,
    )
```

```python
import math

import jax
import jax.numpy as jnp
from jax import lax
from jax.experimental import pallas as pl
from jax.experimental.pallas import tpu as pltpu
from jax.sharding import PartitionSpec as P

LATENT = 512
MAX_BLOCKS = 12
BLOCK_ROWS = 64
REQUESTS = 3
SLOTS = 2
PARTS = 4
LANES = 128
MIB = 1 << 20
STEP = 256

score_scale = 1.0 / math.sqrt(192.0)

VMEM = pl.BlockSpec(memory_space=pltpu.VMEM)
SMEM = pl.BlockSpec(memory_space=pltpu.SMEM)
HBM = pl.BlockSpec(memory_space=pltpu.HBM)
AXES = ("dp", "chip")


def call(kernel, out_shape, in_specs, out_specs, scratch=(), limit=24 * MIB, aliases={}):
    return pl.pallas_call(
        kernel,
        out_shape=out_shape,
        in_specs=in_specs,
        out_specs=out_specs,
        scratch_shapes=scratch,
        input_output_aliases=aliases,
        compiler_params=pltpu.CompilerParams(vmem_limit_bytes=limit),
    )


def dot(a, b, contract=((1,), (0,))):
    return lax.dot_general(a, b, (contract, ((), ())), preferred_element_type=jnp.float32)


def moved_at(source_ref, rank, per_rank):
    first = rank * per_rank
    at = jnp.int32(0)
    for i in range(1, per_rank):
        at = jnp.where(source_ref[first + i] != rank, i, at)
    return at


def iota(shape, dim):
    return lax.broadcasted_iota(jnp.int32, shape, dim)


def send_kernel(source_hbm, ids_hbm, x_hbm, queries_hbm, out_hbm, query_ref, source_ref, ids_ref, x_ref, queries_ref, out_ref, sems):
    pairs = ((ids_hbm, ids_ref), (x_hbm, x_ref), (source_hbm, source_ref), (queries_hbm, queries_ref))
    fetches = [pltpu.make_async_copy(here, there, sems.at[i]) for i, (here, there) in enumerate(pairs)]
    for fetch in fetches:
        fetch.start()
    top, rows = ids_ref.shape
    messages, piece = out_ref.shape
    place_count = SLOTS * PARTS
    ranks = messages // place_count
    columns = PARTS * rows
    shape = (columns, columns)
    before = (iota(shape, 0) // rows == iota(shape, 1) // rows) & (iota(shape, 0) < iota(shape, 1))
    before = before.astype(jnp.bfloat16)
    expert = iota((ranks, columns), 0)
    fetches[0].wait()
    ids = jnp.concatenate([ids_ref[...]] * PARTS, axis=1)
    named = jnp.zeros((ranks, columns), jnp.float32)
    for k in range(top):
        named += (ids[k : k + 1, :] == expert).astype(jnp.float32)
    named = named.astype(jnp.bfloat16)
    slot = jnp.where(named > 0, dot(named, before), -1.0).astype(jnp.bfloat16)
    fetches[1].wait()
    pieces = jnp.concatenate([x_ref[:, p * piece : (p + 1) * piece] for p in range(PARTS)], axis=0)
    steps = 4
    step = messages // steps
    sends = []
    for n in range(steps):
        at = n * step
        spread = ((iota((step, ranks), 0) + at) // place_count == iota((step, ranks), 1)).astype(jnp.bfloat16)
        place = iota((step, columns), 0) % place_count
        hit = (dot(spread, slot) == (place // PARTS).astype(jnp.float32)) & (place % PARTS == iota((step, columns), 1) // rows)
        out_ref[at : at + step, :] = dot(hit.astype(jnp.bfloat16), pieces).astype(jnp.bfloat16)
        sends.append(pltpu.make_async_copy(out_ref.at[pl.ds(at, step)], out_hbm.at[pl.ds(at, step)], sems.at[4 + n]))
        sends[-1].start()
    fetches[2].wait()
    fetches[3].wait()
    query_ref[...] = queries_ref[moved_at(source_ref, lax.axis_index(AXES), REQUESTS)]
    for send in sends:
        send.wait()


def attend(query_cols, cache_rows, length):
    scores = dot(cache_rows, query_cols) * score_scale
    in_range = iota(scores.shape, 0) < length
    row_max = jnp.max(jnp.where(in_range, scores, -1e30), axis=0, keepdims=True)
    weights = jnp.where(in_range, jnp.exp(scores - row_max), 0.0)
    softmax_out = (weights / jnp.sum(weights, axis=0, keepdims=True)).astype(jnp.bfloat16)
    return dot(softmax_out, cache_rows[:, :LATENT], ((0,), (0,))).astype(jnp.bfloat16)


def spread_gates(ids_ref, gates_ref, out_ref):
    rows, top = ids_ref.shape
    messages = out_ref.shape[1]
    place_count = SLOTS * PARTS
    ranks = messages // place_count
    expert = iota((rows, ranks), 1)
    named = jnp.zeros((rows, ranks), jnp.float32)
    rest = jnp.zeros((rows, ranks), jnp.float32)
    for k in range(top):
        chosen = ids_ref[:, k : k + 1] == expert
        named += chosen.astype(jnp.float32)
        rest += jnp.where(chosen, gates_ref[:, k : k + 1], 0.0)
    before = (iota((rows, rows), 1) < iota((rows, rows), 0)).astype(jnp.bfloat16)
    slot = jnp.where(named > 0, dot(before, named.astype(jnp.bfloat16)), -1.0)
    shape = (ranks, messages)
    spread = (iota(shape, 1) // place_count == iota(shape, 0)).astype(jnp.bfloat16)
    place = iota((rows, messages), 1) % place_count
    hit = dot(slot.astype(jnp.bfloat16), spread) == (place // PARTS).astype(jnp.float32)
    for third in range(3):
        head = rest.astype(jnp.bfloat16)
        rest = rest - head.astype(jnp.float32)
        out_ref[third * rows : (third + 1) * rows, :] = jnp.where(hit, dot(head, spread), 0.0).astype(jnp.bfloat16)


def fetch_request(queries_hbm, cache_hbm, first, query_ref, rows_ref, sems):
    start = pl.multiple_of(first * BLOCK_ROWS, BLOCK_ROWS)
    copies = [
        pltpu.make_async_copy(queries_hbm, query_ref, sems.at[0]),
        pltpu.make_async_copy(cache_hbm.at[pl.ds(start, rows_ref.shape[0])], rows_ref, sems.at[1]),
    ]
    for copy in copies:
        copy.start()
    return copies


def own_kernel(
    source_ref, first_ref, tokens_ref, queries_hbm, cache_hbm, ids_ref, gates_ref, attn_ref, spread_ref, query_ref, rows_ref, sems
):
    my_rank = lax.axis_index(AXES)
    mine = moved_at(source_ref, my_rank, REQUESTS)
    own = (jnp.where(mine == 0, 1, 0), jnp.where(mine == 2, 1, 2))
    copies = []
    for i, r in enumerate(own):
        first = first_ref[my_rank * REQUESTS + r]
        copies.append(fetch_request(queries_hbm.at[r], cache_hbm, first, query_ref.at[i], rows_ref.at[i], sems.at[i]))
    spread_gates(ids_ref, gates_ref, spread_ref)
    for i, r in enumerate(own):
        for copy in copies[i]:
            copy.wait()
        attn_ref[r] = attend(query_ref[i], rows_ref[i], tokens_ref[my_rank * REQUESTS + r])
    attn_ref[mine] = jnp.zeros(attn_ref.shape[1:], attn_ref.dtype)


def moved_kernel(source_ref, first_ref, tokens_ref, query_hbm, cache_hbm, out_ref, query_ref, rows_ref, sems):
    next_rank = lax.rem(lax.axis_index(AXES) + 1, source_ref.shape[0] // REQUESTS)
    n = next_rank * REQUESTS + moved_at(source_ref, next_rank, REQUESTS)
    for copy in fetch_request(query_hbm, cache_hbm, first_ref[n], query_ref, rows_ref, sems):
        copy.wait()
    out_ref[...] = attend(query_ref[...], rows_ref[...], tokens_ref[n])


def expert_kernel(x_ref, gate_hbm, up_hbm, down_hbm, out_hbm, gate_ref, up_ref, down_ref, out_ref, wide, flat, hidden, sems):
    messages, piece = x_ref.shape
    units = hidden.shape[1]
    place_count = SLOTS * PARTS
    ranks = messages // place_count
    strips = piece // LANES
    count = 0

    def fetch(here, there, at, width):
        nonlocal count
        columns = pl.ds(at, width)
        copy = pltpu.make_async_copy(here.at[:, columns], there.at[:, columns], sems.at[count])
        copy.start()
        count += 1
        return copy

    near = [(fetch(gate_hbm, gate_ref, n, STEP), fetch(up_hbm, up_ref, n, STEP)) for n in range(0, units, STEP)]
    lows = range(0, piece, STEP)
    far = [[fetch(down_hbm, down_ref, p * piece + low, min(STEP, piece - low)) for p in range(PARTS)] for low in lows]
    for c in range(strips):
        wide[c] = x_ref[:, c * LANES : (c + 1) * LANES].astype(jnp.float32)
    for place in range(place_count):
        s, p = divmod(place, PARTS)
        for c in range(strips):
            at = p * piece + c * LANES
            taken = wide[c, pl.ds(place, ranks, stride=place_count), :]
            flat[s * ranks : (s + 1) * ranks, at : at + LANES] = taken.astype(jnp.bfloat16)
    for n, group in zip(range(0, units, STEP), near):
        for copy in group:
            copy.wait()
        gate_part = dot(flat[...], gate_ref[:, n : n + STEP])
        up_part = dot(flat[...], up_ref[:, n : n + STEP])
        hidden[:, n : n + STEP] = (gate_part / (1.0 + jnp.exp(-gate_part)) * up_part).astype(jnp.bfloat16)
    sends = []
    for low, group in zip(lows, far):
        high = min(low + STEP, piece)
        for copy in group:
            copy.wait()
        for p in range(PARTS):
            result = dot(hidden[...], down_ref[:, p * piece + low : p * piece + high])
            for s in range(SLOTS):
                for c in range(low // LANES, high // LANES):
                    at = c * LANES - low
                    kept = result[s * ranks : (s + 1) * ranks, at : at + LANES]
                    wide[c, pl.ds(s * PARTS + p, ranks, stride=place_count), :] = kept
        for c in range(low // LANES, high // LANES):
            out_ref[:, c * LANES : (c + 1) * LANES] = wide[c].astype(jnp.bfloat16)
        columns = pl.ds(low, high - low)
        sends.append(pltpu.make_async_copy(out_ref.at[:, columns], out_hbm.at[:, columns], sems.at[count + len(sends)]))
        sends[-1].start()
    for send in sends:
        send.wait()


def combine_kernel(source_ref, gates_ref, returned_ref, moved_ref, attn_hbm, out_ref, attn_out_hbm, sem):
    del attn_hbm
    mine = moved_at(source_ref, lax.axis_index(AXES), REQUESTS)
    copy = pltpu.make_async_copy(moved_ref, attn_out_hbm.at[mine], sem)
    copy.start()
    rows = out_ref.shape[0]
    piece = returned_ref.shape[1]
    gates = gates_ref[...]
    part = iota(gates.shape, 1) % PARTS
    split = jnp.concatenate([jnp.where(part == p, gates, jnp.zeros_like(gates)) for p in range(PARTS)], axis=0)
    total = dot(split, returned_ref[...])
    for p in range(PARTS):
        thirds = [total[(p * 3 + third) * rows : (p * 3 + third + 1) * rows] for third in range(3)]
        out_ref[:, p * piece : (p + 1) * piece] = (thirds[0] + thirds[1] + thirds[2]).astype(jnp.bfloat16)
    copy.wait()


def per_device(
    moe_in,
    expert_ids,
    expert_gates,
    gate_weight,
    up_weight,
    down_weight,
    queries,
    cache_pool,
    req_source,
    req_first,
    req_tokens,
):
    group_size = lax.axis_size(AXES)
    row_count, model_width = moe_in.shape
    place_count = SLOTS * PARTS
    messages = group_size * place_count
    piece = model_width // PARTS
    units = gate_weight.shape[2]
    heads, features = queries.shape[1:]
    bf16 = jnp.bfloat16
    dma = pltpu.SemaphoreType.DMA

    def exchange(x):
        x = x.reshape(group_size, place_count, piece)
        return lax.all_to_all(x, AXES, split_axis=0, concat_axis=0, tiled=True).reshape(messages, piece)

    def to_rank(x, distance):
        return lax.ppermute(x, AXES, [(i, (i + distance) % group_size) for i in range(group_size)])

    def stay(*arrays):
        return [pltpu.with_memory_space_constraint(x, pltpu.HBM) for x in arrays]

    message = (messages, piece)
    query_cols = jnp.swapaxes(queries, 1, 2)
    cache_rows = cache_pool.reshape(-1, features)
    outgoing, moved_query = call(
        send_kernel,
        (pltpu.HBM(message, bf16), jax.ShapeDtypeStruct((features, heads), bf16)),
        [HBM] * 4,
        (HBM, VMEM),
        [
            pltpu.SMEM(req_source.shape, jnp.int32),
            pltpu.VMEM(expert_ids.shape[::-1], jnp.int32),
            pltpu.VMEM(moe_in.shape, bf16),
            pltpu.VMEM(query_cols.shape, bf16),
            pltpu.VMEM(message, bf16),
            dma((8,)),
        ],
    )(*stay(req_source, expert_ids.T, moe_in, query_cols))
    moved_query = to_rank(moved_query, -1)
    arrived = exchange(outgoing)

    plan = (req_source, req_first, req_tokens)
    answered = call(
        expert_kernel,
        pltpu.HBM(message, bf16),
        [VMEM] + [HBM] * 3,
        HBM,
        [
            pltpu.VMEM(gate_weight.shape[1:], bf16),
            pltpu.VMEM(up_weight.shape[1:], bf16),
            pltpu.VMEM(down_weight.shape[1:], bf16),
            pltpu.VMEM(message, bf16),
            pltpu.VMEM((piece // LANES, messages, LANES), jnp.float32),
            pltpu.VMEM((SLOTS * group_size, model_width), bf16),
            pltpu.VMEM((SLOTS * group_size, units), bf16),
            dma((2 * (units // STEP) + (PARTS + 1) * -(-piece // STEP),)),
        ],
        limit=44 * MIB,
    )(arrived, *stay(gate_weight[0], up_weight[0], down_weight[0]))
    answered, moved_query, query_cols, cache_rows = lax.optimization_barrier((answered, moved_query, query_cols, cache_rows))
    returned = exchange(answered)
    attn_own, gates = call(
        own_kernel,
        (
            jax.ShapeDtypeStruct((REQUESTS, heads, LATENT), bf16),
            jax.ShapeDtypeStruct((3 * row_count, messages), bf16),
        ),
        [SMEM] * 3 + [HBM] * 2 + [VMEM] * 2,
        (VMEM,) * 2,
        [
            pltpu.VMEM((REQUESTS - 1, features, heads), bf16),
            pltpu.VMEM((REQUESTS - 1, MAX_BLOCKS * BLOCK_ROWS, features), bf16),
            dma((REQUESTS - 1, 2)),
        ],
    )(*plan, *stay(query_cols, cache_rows), expert_ids, expert_gates)
    moved_out = call(
        moved_kernel,
        jax.ShapeDtypeStruct((heads, LATENT), bf16),
        [SMEM] * 3 + [HBM] * 2,
        VMEM,
        [
            pltpu.VMEM((features, heads), bf16),
            pltpu.VMEM((MAX_BLOCKS * BLOCK_ROWS, features), bf16),
            dma((2,)),
        ],
    )(*plan, moved_query, *stay(cache_rows))
    moved_out = to_rank(moved_out, 1)
    moe_out, attn_latent = call(
        combine_kernel,
        (jax.ShapeDtypeStruct(moe_in.shape, bf16), pltpu.HBM(attn_own.shape, bf16)),
        [SMEM] + [VMEM] * 3 + [HBM],
        (VMEM, HBM),
        [dma],
        aliases={4: 1},
    )(req_source, gates, returned, moved_out, *stay(attn_own))
    return (moe_out, attn_latent)


def solution(mesh):
    rows = P(("dp", "chip"), None)
    blocks = P(("dp", "chip"), None, None)
    return jax.shard_map(
        per_device,
        mesh=mesh,
        in_specs=(rows, rows, rows, blocks, blocks, blocks, blocks, blocks, P(), P(), P()),
        out_specs=(rows, blocks),
        check_vma=False,
    )
```

```python
import math

import jax
import jax.numpy as jnp
from jax import lax
from jax.experimental import pallas as pl
from jax.experimental.pallas import tpu as pltpu
from jax.sharding import PartitionSpec as P

LATENT = 512
MAX_BLOCKS = 12
BLOCK_ROWS = 64
REQUESTS = 3
SLOTS = 2
PARTS = 4
LANES = 128
MIB = 1 << 20
STEP = 256
AHEAD = pl.CostEstimate(flops=20_000_000_000, transcendentals=0, bytes_accessed=40_000_000)

score_scale = 1.0 / math.sqrt(192.0)

VMEM = pl.BlockSpec(memory_space=pltpu.VMEM)
SMEM = pl.BlockSpec(memory_space=pltpu.SMEM)
HBM = pl.BlockSpec(memory_space=pltpu.HBM)
AXES = ("dp", "chip")


def call(kernel, out_shape, in_specs, out_specs, scratch=(), limit=24 * MIB, aliases={}, cost=None):
    return pl.pallas_call(
        kernel,
        out_shape=out_shape,
        in_specs=in_specs,
        out_specs=out_specs,
        scratch_shapes=scratch,
        input_output_aliases=aliases,
        cost_estimate=cost,
        compiler_params=pltpu.CompilerParams(vmem_limit_bytes=limit),
    )


def dot(a, b, contract=((1,), (0,))):
    return lax.dot_general(a, b, (contract, ((), ())), preferred_element_type=jnp.float32)


def moved_at(source_ref, rank, per_rank):
    first = rank * per_rank
    at = jnp.int32(0)
    for i in range(1, per_rank):
        at = jnp.where(source_ref[first + i] != rank, i, at)
    return at


def iota(shape, dim):
    return lax.broadcasted_iota(jnp.int32, shape, dim)


def send_kernel(source_hbm, ids_hbm, x_hbm, queries_hbm, out_ref, query_ref, source_ref, ids_ref, x_ref, queries_ref, sems):
    pairs = ((ids_hbm, ids_ref), (x_hbm, x_ref), (source_hbm, source_ref), (queries_hbm, queries_ref))
    fetches = [pltpu.make_async_copy(here, there, sems.at[i]) for i, (here, there) in enumerate(pairs)]
    for fetch in fetches:
        fetch.start()
    top, rows = ids_ref.shape
    messages, piece = out_ref.shape
    place_count = SLOTS * PARTS
    ranks = messages // place_count
    columns = PARTS * rows
    shape = (columns, columns)
    before = (iota(shape, 0) // rows == iota(shape, 1) // rows) & (iota(shape, 0) < iota(shape, 1))
    before = before.astype(jnp.bfloat16)
    expert = iota((ranks, columns), 0)
    fetches[0].wait()
    ids = jnp.concatenate([ids_ref[...]] * PARTS, axis=1)
    named = jnp.zeros((ranks, columns), jnp.float32)
    for k in range(top):
        named += (ids[k : k + 1, :] == expert).astype(jnp.float32)
    named = named.astype(jnp.bfloat16)
    slot = jnp.where(named > 0, dot(named, before), -1.0).astype(jnp.bfloat16)
    fetches[1].wait()
    pieces = jnp.concatenate([x_ref[:, p * piece : (p + 1) * piece] for p in range(PARTS)], axis=0)
    steps = 4
    step = messages // steps
    for n in range(steps):
        at = n * step
        spread = ((iota((step, ranks), 0) + at) // place_count == iota((step, ranks), 1)).astype(jnp.bfloat16)
        place = iota((step, columns), 0) % place_count
        hit = (dot(spread, slot) == (place // PARTS).astype(jnp.float32)) & (place % PARTS == iota((step, columns), 1) // rows)
        out_ref[at : at + step, :] = dot(hit.astype(jnp.bfloat16), pieces).astype(jnp.bfloat16)
    fetches[2].wait()
    fetches[3].wait()
    query_ref[...] = queries_ref[moved_at(source_ref, lax.axis_index(AXES), REQUESTS)]


def attend(query_cols, cache_rows, length):
    scores = dot(cache_rows, query_cols) * score_scale
    in_range = iota(scores.shape, 0) < length
    row_max = jnp.max(jnp.where(in_range, scores, -1e30), axis=0, keepdims=True)
    weights = jnp.where(in_range, jnp.exp(scores - row_max), 0.0)
    softmax_out = (weights / jnp.sum(weights, axis=0, keepdims=True)).astype(jnp.bfloat16)
    return dot(softmax_out, cache_rows[:, :LATENT], ((0,), (0,))).astype(jnp.bfloat16)


def spread_gates(ids_ref, gates_ref, out_ref):
    rows, top = ids_ref.shape
    messages = out_ref.shape[1]
    place_count = SLOTS * PARTS
    ranks = messages // place_count
    expert = iota((rows, ranks), 1)
    named = jnp.zeros((rows, ranks), jnp.float32)
    rest = jnp.zeros((rows, ranks), jnp.float32)
    for k in range(top):
        chosen = ids_ref[:, k : k + 1] == expert
        named += chosen.astype(jnp.float32)
        rest += jnp.where(chosen, gates_ref[:, k : k + 1], 0.0)
    before = (iota((rows, rows), 1) < iota((rows, rows), 0)).astype(jnp.bfloat16)
    slot = jnp.where(named > 0, dot(before, named.astype(jnp.bfloat16)), -1.0)
    shape = (ranks, messages)
    spread = (iota(shape, 1) // place_count == iota(shape, 0)).astype(jnp.bfloat16)
    place = iota((rows, messages), 1) % place_count
    hit = dot(slot.astype(jnp.bfloat16), spread) == (place // PARTS).astype(jnp.float32)
    for third in range(3):
        head = rest.astype(jnp.bfloat16)
        rest = rest - head.astype(jnp.float32)
        out_ref[third * rows : (third + 1) * rows, :] = jnp.where(hit, dot(head, spread), 0.0).astype(jnp.bfloat16)


def fetch_request(queries_hbm, cache_hbm, first, query_ref, rows_ref, sems):
    start = pl.multiple_of(first * BLOCK_ROWS, BLOCK_ROWS)
    copies = [
        pltpu.make_async_copy(queries_hbm, query_ref, sems.at[0]),
        pltpu.make_async_copy(cache_hbm.at[pl.ds(start, rows_ref.shape[0])], rows_ref, sems.at[1]),
    ]
    for copy in copies:
        copy.start()
    return copies


def own_kernel(
    source_ref, first_ref, tokens_ref, queries_hbm, cache_hbm, ids_ref, gates_ref, attn_ref, spread_ref, query_ref, rows_ref, sems
):
    my_rank = lax.axis_index(AXES)
    mine = moved_at(source_ref, my_rank, REQUESTS)
    own = (jnp.where(mine == 0, 1, 0), jnp.where(mine == 2, 1, 2))
    copies = []
    for i, r in enumerate(own):
        first = first_ref[my_rank * REQUESTS + r]
        copies.append(fetch_request(queries_hbm.at[r], cache_hbm, first, query_ref.at[i], rows_ref.at[i], sems.at[i]))
    spread_gates(ids_ref, gates_ref, spread_ref)
    for i, r in enumerate(own):
        for copy in copies[i]:
            copy.wait()
        attn_ref[r] = attend(query_ref[i], rows_ref[i], tokens_ref[my_rank * REQUESTS + r])
    attn_ref[mine] = jnp.zeros(attn_ref.shape[1:], attn_ref.dtype)


def moved_kernel(source_ref, first_ref, tokens_ref, query_hbm, cache_hbm, out_ref, query_ref, rows_ref, sems):
    next_rank = lax.rem(lax.axis_index(AXES) + 1, source_ref.shape[0] // REQUESTS)
    n = next_rank * REQUESTS + moved_at(source_ref, next_rank, REQUESTS)
    for copy in fetch_request(query_hbm, cache_hbm, first_ref[n], query_ref, rows_ref, sems):
        copy.wait()
    out_ref[...] = attend(query_ref[...], rows_ref[...], tokens_ref[n])


def expert_kernel(x_ref, gate_ref, up_ref, down_ref, out_hbm, out_ref, wide, flat, hidden, sems):
    messages, piece = x_ref.shape
    units = hidden.shape[1]
    place_count = SLOTS * PARTS
    ranks = messages // place_count
    strips = piece // LANES
    lows = range(0, piece, STEP)
    for c in range(strips):
        wide[c] = x_ref[:, c * LANES : (c + 1) * LANES].astype(jnp.float32)
    for place in range(place_count):
        s, p = divmod(place, PARTS)
        for c in range(strips):
            at = p * piece + c * LANES
            taken = wide[c, pl.ds(place, ranks, stride=place_count), :]
            flat[s * ranks : (s + 1) * ranks, at : at + LANES] = taken.astype(jnp.bfloat16)
    for n in range(0, units, STEP):
        gate_part = dot(flat[...], gate_ref[:, n : n + STEP])
        up_part = dot(flat[...], up_ref[:, n : n + STEP])
        hidden[:, n : n + STEP] = (gate_part / (1.0 + jnp.exp(-gate_part)) * up_part).astype(jnp.bfloat16)
    sends = []
    for low in lows:
        high = min(low + STEP, piece)
        for p in range(PARTS):
            result = dot(hidden[...], down_ref[:, p * piece + low : p * piece + high])
            for s in range(SLOTS):
                for c in range(low // LANES, high // LANES):
                    at = c * LANES - low
                    kept = result[s * ranks : (s + 1) * ranks, at : at + LANES]
                    wide[c, pl.ds(s * PARTS + p, ranks, stride=place_count), :] = kept
        for c in range(low // LANES, high // LANES):
            out_ref[:, c * LANES : (c + 1) * LANES] = wide[c].astype(jnp.bfloat16)
        columns = pl.ds(low, high - low)
        sends.append(pltpu.make_async_copy(out_ref.at[:, columns], out_hbm.at[:, columns], sems.at[len(sends)]))
        sends[-1].start()
    for send in sends:
        send.wait()


def combine_kernel(source_ref, gates_ref, returned_ref, moved_ref, attn_hbm, out_ref, attn_out_hbm, sem):
    del attn_hbm
    mine = moved_at(source_ref, lax.axis_index(AXES), REQUESTS)
    copy = pltpu.make_async_copy(moved_ref, attn_out_hbm.at[mine], sem)
    copy.start()
    rows = out_ref.shape[0]
    piece = returned_ref.shape[1]
    gates = gates_ref[...]
    part = iota(gates.shape, 1) % PARTS
    split = jnp.concatenate([jnp.where(part == p, gates, jnp.zeros_like(gates)) for p in range(PARTS)], axis=0)
    total = dot(split, returned_ref[...])
    for p in range(PARTS):
        thirds = [total[(p * 3 + third) * rows : (p * 3 + third + 1) * rows] for third in range(3)]
        out_ref[:, p * piece : (p + 1) * piece] = (thirds[0] + thirds[1] + thirds[2]).astype(jnp.bfloat16)
    copy.wait()


def per_device(
    moe_in,
    expert_ids,
    expert_gates,
    gate_weight,
    up_weight,
    down_weight,
    queries,
    cache_pool,
    req_source,
    req_first,
    req_tokens,
):
    group_size = lax.axis_size(AXES)
    row_count, model_width = moe_in.shape
    place_count = SLOTS * PARTS
    messages = group_size * place_count
    piece = model_width // PARTS
    units = gate_weight.shape[2]
    heads, features = queries.shape[1:]
    bf16 = jnp.bfloat16
    dma = pltpu.SemaphoreType.DMA

    def exchange(x):
        x = x.reshape(group_size, place_count, piece)
        return lax.all_to_all(x, AXES, split_axis=0, concat_axis=0, tiled=True).reshape(messages, piece)

    def to_rank(x, distance):
        return lax.ppermute(x, AXES, [(i, (i + distance) % group_size) for i in range(group_size)])

    def stay(*arrays):
        return [pltpu.with_memory_space_constraint(x, pltpu.HBM) for x in arrays]

    message = (messages, piece)
    query_cols = jnp.swapaxes(queries, 1, 2)
    cache_rows = cache_pool.reshape(-1, features)
    outgoing, moved_query = call(
        send_kernel,
        (jax.ShapeDtypeStruct(message, bf16), jax.ShapeDtypeStruct((features, heads), bf16)),
        [HBM] * 4,
        (VMEM, VMEM),
        [
            pltpu.SMEM(req_source.shape, jnp.int32),
            pltpu.VMEM(expert_ids.shape[::-1], jnp.int32),
            pltpu.VMEM(moe_in.shape, bf16),
            pltpu.VMEM(query_cols.shape, bf16),
            dma((4,)),
        ],
        cost=AHEAD,
    )(*stay(req_source, expert_ids.T, moe_in, query_cols))
    arrived = exchange(outgoing)
    arrived, moved_query = lax.optimization_barrier((arrived, moved_query))
    moved_query = to_rank(moved_query, -1)

    plan = (req_source, req_first, req_tokens)
    answered = call(
        expert_kernel,
        pltpu.HBM(message, bf16),
        [VMEM] * 4,
        HBM,
        [
            pltpu.VMEM(message, bf16),
            pltpu.VMEM((piece // LANES, messages, LANES), jnp.float32),
            pltpu.VMEM((SLOTS * group_size, model_width), bf16),
            pltpu.VMEM((SLOTS * group_size, units), bf16),
            dma((-(-piece // STEP),)),
        ],
        limit=16 * MIB,
    )(arrived, *[pltpu.with_memory_space_constraint(w[0], pltpu.VMEM) for w in (gate_weight, up_weight, down_weight)])
    answered, moved_query, query_cols, cache_rows = lax.optimization_barrier((answered, moved_query, query_cols, cache_rows))
    returned = exchange(answered)
    attn_own, gates = call(
        own_kernel,
        (
            jax.ShapeDtypeStruct((REQUESTS, heads, LATENT), bf16),
            jax.ShapeDtypeStruct((3 * row_count, messages), bf16),
        ),
        [SMEM] * 3 + [HBM] * 2 + [VMEM] * 2,
        (VMEM,) * 2,
        [
            pltpu.VMEM((REQUESTS - 1, features, heads), bf16),
            pltpu.VMEM((REQUESTS - 1, MAX_BLOCKS * BLOCK_ROWS, features), bf16),
            dma((REQUESTS - 1, 2)),
        ],
    )(*plan, *stay(query_cols, cache_rows), expert_ids, expert_gates)
    moved_out = call(
        moved_kernel,
        jax.ShapeDtypeStruct((heads, LATENT), bf16),
        [SMEM] * 3 + [HBM] * 2,
        VMEM,
        [
            pltpu.VMEM((features, heads), bf16),
            pltpu.VMEM((MAX_BLOCKS * BLOCK_ROWS, features), bf16),
            dma((2,)),
        ],
    )(*plan, moved_query, *stay(cache_rows))
    moved_out = to_rank(moved_out, 1)
    moe_out, attn_latent = call(
        combine_kernel,
        (jax.ShapeDtypeStruct(moe_in.shape, bf16), pltpu.HBM(attn_own.shape, bf16)),
        [SMEM] + [VMEM] * 3 + [HBM],
        (VMEM, HBM),
        [dma],
        aliases={4: 1},
    )(req_source, gates, returned, moved_out, *stay(attn_own))
    return (moe_out, attn_latent)


def solution(mesh):
    rows = P(("dp", "chip"), None)
    blocks = P(("dp", "chip"), None, None)
    return jax.shard_map(
        per_device,
        mesh=mesh,
        in_specs=(rows, rows, rows, blocks, blocks, blocks, blocks, blocks, P(), P(), P()),
        out_specs=(rows, blocks),
        check_vma=False,
    )
```

```python
import math

import jax
import jax.numpy as jnp
from jax import lax
from jax.experimental import pallas as pl
from jax.experimental.pallas import tpu as pltpu
from jax.sharding import PartitionSpec as P

LATENT = 512
MAX_BLOCKS = 12
BLOCK_ROWS = 64
REQUESTS = 3
SLOTS = 2
PARTS = 4
LANES = 128
MIB = 1 << 20
STEP = 256
AHEAD = pl.CostEstimate(flops=20_000_000_000, transcendentals=0, bytes_accessed=40_000_000)

score_scale = 1.0 / math.sqrt(192.0)

VMEM = pl.BlockSpec(memory_space=pltpu.VMEM)
SMEM = pl.BlockSpec(memory_space=pltpu.SMEM)
HBM = pl.BlockSpec(memory_space=pltpu.HBM)
AXES = ("dp", "chip")


def call(kernel, out_shape, in_specs, out_specs, scratch=(), limit=24 * MIB, aliases={}, cost=None):
    return pl.pallas_call(
        kernel,
        out_shape=out_shape,
        in_specs=in_specs,
        out_specs=out_specs,
        scratch_shapes=scratch,
        input_output_aliases=aliases,
        cost_estimate=cost,
        compiler_params=pltpu.CompilerParams(vmem_limit_bytes=limit),
    )


def dot(a, b, contract=((1,), (0,))):
    return lax.dot_general(a, b, (contract, ((), ())), preferred_element_type=jnp.float32)


def moved_at(source_ref, rank, per_rank):
    first = rank * per_rank
    at = jnp.int32(0)
    for i in range(1, per_rank):
        at = jnp.where(source_ref[first + i] != rank, i, at)
    return at


def iota(shape, dim):
    return lax.broadcasted_iota(jnp.int32, shape, dim)


def send_kernel(source_hbm, ids_hbm, x_hbm, queries_hbm, out_ref, query_ref, source_ref, ids_ref, x_ref, queries_ref, sems):
    pairs = ((ids_hbm, ids_ref), (x_hbm, x_ref), (source_hbm, source_ref), (queries_hbm, queries_ref))
    fetches = [pltpu.make_async_copy(here, there, sems.at[i]) for i, (here, there) in enumerate(pairs)]
    for fetch in fetches:
        fetch.start()
    top, rows = ids_ref.shape
    messages, piece = out_ref.shape
    place_count = SLOTS * PARTS
    ranks = messages // place_count
    columns = PARTS * rows
    shape = (columns, columns)
    before = (iota(shape, 0) // rows == iota(shape, 1) // rows) & (iota(shape, 0) < iota(shape, 1))
    before = before.astype(jnp.bfloat16)
    expert = iota((ranks, columns), 0)
    spread = (iota((messages, ranks), 0) // place_count == iota((messages, ranks), 1)).astype(jnp.bfloat16)
    place = iota((messages, columns), 0) % place_count
    same_part = place % PARTS == iota((messages, columns), 1) // rows
    wanted = jnp.where(same_part, (place // PARTS).astype(jnp.float32), float(SLOTS))
    fetches[0].wait()
    ids = jnp.concatenate([ids_ref[...]] * PARTS, axis=1)
    named = jnp.zeros((ranks, columns), jnp.float32)
    for k in range(top):
        named += (ids[k : k + 1, :] == expert).astype(jnp.float32)
    named = named.astype(jnp.bfloat16)
    slot = jnp.where(named > 0, dot(named, before), -1.0).astype(jnp.bfloat16)
    hit = (dot(spread, slot) == wanted).astype(jnp.bfloat16)
    fetches[1].wait()
    pieces = jnp.concatenate([x_ref[:, p * piece : (p + 1) * piece] for p in range(PARTS)], axis=0)
    out_ref[...] = dot(hit, pieces).astype(jnp.bfloat16)
    fetches[2].wait()
    fetches[3].wait()
    query_ref[...] = queries_ref[moved_at(source_ref, lax.axis_index(AXES), REQUESTS)]


def attend(query_cols, cache_rows, length):
    scores = dot(cache_rows, query_cols) * score_scale
    in_range = iota(scores.shape, 0) < length
    row_max = jnp.max(jnp.where(in_range, scores, -1e30), axis=0, keepdims=True)
    weights = jnp.where(in_range, jnp.exp(scores - row_max), 0.0)
    softmax_out = (weights / jnp.sum(weights, axis=0, keepdims=True)).astype(jnp.bfloat16)
    return dot(softmax_out, cache_rows[:, :LATENT], ((0,), (0,))).astype(jnp.bfloat16)


def spread_gates(ids_ref, gates_ref, out_ref):
    rows, top = ids_ref.shape
    messages = out_ref.shape[1]
    place_count = SLOTS * PARTS
    ranks = messages // place_count
    expert = iota((rows, ranks), 1)
    named = jnp.zeros((rows, ranks), jnp.float32)
    rest = jnp.zeros((rows, ranks), jnp.float32)
    for k in range(top):
        chosen = ids_ref[:, k : k + 1] == expert
        named += chosen.astype(jnp.float32)
        rest += jnp.where(chosen, gates_ref[:, k : k + 1], 0.0)
    before = (iota((rows, rows), 1) < iota((rows, rows), 0)).astype(jnp.bfloat16)
    slot = jnp.where(named > 0, dot(before, named.astype(jnp.bfloat16)), -1.0)
    shape = (ranks, messages)
    spread = (iota(shape, 1) // place_count == iota(shape, 0)).astype(jnp.bfloat16)
    place = iota((rows, messages), 1) % place_count
    hit = dot(slot.astype(jnp.bfloat16), spread) == (place // PARTS).astype(jnp.float32)
    for third in range(3):
        head = rest.astype(jnp.bfloat16)
        rest = rest - head.astype(jnp.float32)
        out_ref[third * rows : (third + 1) * rows, :] = jnp.where(hit, dot(head, spread), 0.0).astype(jnp.bfloat16)


def fetch_request(queries_hbm, cache_hbm, first, query_ref, rows_ref, sems):
    start = pl.multiple_of(first * BLOCK_ROWS, BLOCK_ROWS)
    copies = [
        pltpu.make_async_copy(queries_hbm, query_ref, sems.at[0]),
        pltpu.make_async_copy(cache_hbm.at[pl.ds(start, rows_ref.shape[0])], rows_ref, sems.at[1]),
    ]
    for copy in copies:
        copy.start()
    return copies


def own_kernel(
    source_ref, first_ref, tokens_ref, queries_hbm, cache_hbm, ids_ref, gates_ref, attn_ref, spread_ref, query_ref, rows_ref, sems
):
    my_rank = lax.axis_index(AXES)
    mine = moved_at(source_ref, my_rank, REQUESTS)
    own = (jnp.where(mine == 0, 1, 0), jnp.where(mine == 2, 1, 2))
    copies = []
    for i, r in enumerate(own):
        first = first_ref[my_rank * REQUESTS + r]
        copies.append(fetch_request(queries_hbm.at[r], cache_hbm, first, query_ref.at[i], rows_ref.at[i], sems.at[i]))
    spread_gates(ids_ref, gates_ref, spread_ref)
    for i, r in enumerate(own):
        for copy in copies[i]:
            copy.wait()
        attn_ref[r] = attend(query_ref[i], rows_ref[i], tokens_ref[my_rank * REQUESTS + r])
    attn_ref[mine] = jnp.zeros(attn_ref.shape[1:], attn_ref.dtype)


def moved_kernel(source_ref, first_ref, tokens_ref, query_hbm, cache_hbm, out_ref, query_ref, rows_ref, sems):
    next_rank = lax.rem(lax.axis_index(AXES) + 1, source_ref.shape[0] // REQUESTS)
    n = next_rank * REQUESTS + moved_at(source_ref, next_rank, REQUESTS)
    for copy in fetch_request(query_hbm, cache_hbm, first_ref[n], query_ref, rows_ref, sems):
        copy.wait()
    out_ref[...] = attend(query_ref[...], rows_ref[...], tokens_ref[n])


def expert_kernel(x_ref, gate_ref, up_ref, down_ref, out_hbm, out_ref, wide, flat, hidden, sems):
    messages, piece = x_ref.shape
    units = hidden.shape[1]
    place_count = SLOTS * PARTS
    ranks = messages // place_count
    strips = piece // LANES
    lows = range(0, piece, STEP)
    for c in range(strips):
        wide[c] = x_ref[:, c * LANES : (c + 1) * LANES].astype(jnp.float32)
    for place in range(place_count):
        s, p = divmod(place, PARTS)
        for c in range(strips):
            at = p * piece + c * LANES
            taken = wide[c, pl.ds(place, ranks, stride=place_count), :]
            flat[s * ranks : (s + 1) * ranks, at : at + LANES] = taken.astype(jnp.bfloat16)
    for n in range(0, units, STEP):
        gate_part = dot(flat[...], gate_ref[:, n : n + STEP])
        up_part = dot(flat[...], up_ref[:, n : n + STEP])
        hidden[:, n : n + STEP] = (gate_part / (1.0 + jnp.exp(-gate_part)) * up_part).astype(jnp.bfloat16)
    sends = []
    for low in lows:
        high = min(low + STEP, piece)
        for p in range(PARTS):
            result = dot(hidden[...], down_ref[:, p * piece + low : p * piece + high])
            for s in range(SLOTS):
                for c in range(low // LANES, high // LANES):
                    at = c * LANES - low
                    kept = result[s * ranks : (s + 1) * ranks, at : at + LANES]
                    wide[c, pl.ds(s * PARTS + p, ranks, stride=place_count), :] = kept
        for c in range(low // LANES, high // LANES):
            out_ref[:, c * LANES : (c + 1) * LANES] = wide[c].astype(jnp.bfloat16)
        columns = pl.ds(low, high - low)
        sends.append(pltpu.make_async_copy(out_ref.at[:, columns], out_hbm.at[:, columns], sems.at[len(sends)]))
        sends[-1].start()
    for send in sends:
        send.wait()


def combine_kernel(source_hbm, gates_ref, returned_ref, moved_ref, attn_hbm, out_hbm, attn_out_hbm, source_ref, out_ref, sems):
    del attn_hbm
    fetch = pltpu.make_async_copy(source_hbm, source_ref, sems.at[0])
    fetch.start()
    rows = out_ref.shape[0]
    piece = returned_ref.shape[1]
    gates = gates_ref[...]
    part = iota(gates.shape, 1) % PARTS
    split = jnp.concatenate([jnp.where(part == p, gates, jnp.zeros_like(gates)) for p in range(PARTS)], axis=0)
    total = dot(split, returned_ref[...])
    for p in range(PARTS):
        thirds = [total[(p * 3 + third) * rows : (p * 3 + third + 1) * rows] for third in range(3)]
        out_ref[:, p * piece : (p + 1) * piece] = (thirds[0] + thirds[1] + thirds[2]).astype(jnp.bfloat16)
    out_copy = pltpu.make_async_copy(out_ref, out_hbm, sems.at[1])
    out_copy.start()
    fetch.wait()
    mine = moved_at(source_ref, lax.axis_index(AXES), REQUESTS)
    attn_copy = pltpu.make_async_copy(moved_ref, attn_out_hbm.at[mine], sems.at[2])
    attn_copy.start()
    out_copy.wait()
    attn_copy.wait()


def per_device(
    moe_in,
    expert_ids,
    expert_gates,
    gate_weight,
    up_weight,
    down_weight,
    queries,
    cache_pool,
    req_source,
    req_first,
    req_tokens,
):
    group_size = lax.axis_size(AXES)
    row_count, model_width = moe_in.shape
    place_count = SLOTS * PARTS
    messages = group_size * place_count
    piece = model_width // PARTS
    units = gate_weight.shape[2]
    heads, features = queries.shape[1:]
    bf16 = jnp.bfloat16
    dma = pltpu.SemaphoreType.DMA

    def exchange(x):
        x = x.reshape(group_size, place_count, piece)
        return lax.all_to_all(x, AXES, split_axis=0, concat_axis=0, tiled=True).reshape(messages, piece)

    def to_rank(x, distance):
        return lax.ppermute(x, AXES, [(i, (i + distance) % group_size) for i in range(group_size)])

    def stay(*arrays):
        return [pltpu.with_memory_space_constraint(x, pltpu.HBM) for x in arrays]

    message = (messages, piece)
    query_cols = jnp.swapaxes(queries, 1, 2)
    cache_rows = cache_pool.reshape(-1, features)
    outgoing, moved_query = call(
        send_kernel,
        (jax.ShapeDtypeStruct(message, bf16), jax.ShapeDtypeStruct((features, heads), bf16)),
        [HBM] * 4,
        (VMEM, VMEM),
        [
            pltpu.SMEM(req_source.shape, jnp.int32),
            pltpu.VMEM(expert_ids.shape[::-1], jnp.int32),
            pltpu.VMEM(moe_in.shape, bf16),
            pltpu.VMEM(query_cols.shape, bf16),
            dma((4,)),
        ],
        cost=AHEAD,
    )(*stay(req_source, expert_ids.T, moe_in, query_cols))
    arrived = exchange(outgoing)
    arrived, moved_query = lax.optimization_barrier((arrived, moved_query))
    moved_query = to_rank(moved_query, -1)

    plan = (req_source, req_first, req_tokens)
    answered = call(
        expert_kernel,
        pltpu.HBM(message, bf16),
        [VMEM] * 4,
        HBM,
        [
            pltpu.VMEM(message, bf16),
            pltpu.VMEM((piece // LANES, messages, LANES), jnp.float32),
            pltpu.VMEM((SLOTS * group_size, model_width), bf16),
            pltpu.VMEM((SLOTS * group_size, units), bf16),
            dma((-(-piece // STEP),)),
        ],
        limit=16 * MIB,
    )(arrived, *[pltpu.with_memory_space_constraint(w[0], pltpu.VMEM) for w in (gate_weight, up_weight, down_weight)])
    answered, moved_query, query_cols, cache_rows = lax.optimization_barrier((answered, moved_query, query_cols, cache_rows))
    returned = exchange(answered)
    attn_own, gates = call(
        own_kernel,
        (
            jax.ShapeDtypeStruct((REQUESTS, heads, LATENT), bf16),
            jax.ShapeDtypeStruct((3 * row_count, messages), bf16),
        ),
        [SMEM] * 3 + [HBM] * 2 + [VMEM] * 2,
        (VMEM,) * 2,
        [
            pltpu.VMEM((REQUESTS - 1, features, heads), bf16),
            pltpu.VMEM((REQUESTS - 1, MAX_BLOCKS * BLOCK_ROWS, features), bf16),
            dma((REQUESTS - 1, 2)),
        ],
    )(*plan, *stay(query_cols, cache_rows), expert_ids, expert_gates)
    moved_out = call(
        moved_kernel,
        jax.ShapeDtypeStruct((heads, LATENT), bf16),
        [SMEM] * 3 + [HBM] * 2,
        VMEM,
        [
            pltpu.VMEM((features, heads), bf16),
            pltpu.VMEM((MAX_BLOCKS * BLOCK_ROWS, features), bf16),
            dma((2,)),
        ],
    )(*plan, moved_query, *stay(cache_rows))
    moved_out = to_rank(moved_out, 1)
    moe_out, attn_latent = call(
        combine_kernel,
        (pltpu.HBM(moe_in.shape, bf16), pltpu.HBM(attn_own.shape, bf16)),
        [HBM] + [VMEM] * 3 + [HBM],
        (HBM, HBM),
        [pltpu.SMEM(req_source.shape, jnp.int32), pltpu.VMEM(moe_in.shape, bf16), dma((3,))],
        aliases={4: 1},
    )(*stay(req_source), gates, returned, moved_out, *stay(attn_own))
    return (moe_out, attn_latent)


def solution(mesh):
    rows = P(("dp", "chip"), None)
    blocks = P(("dp", "chip"), None, None)
    return jax.shard_map(
        per_device,
        mesh=mesh,
        in_specs=(rows, rows, rows, blocks, blocks, blocks, blocks, blocks, P(), P(), P()),
        out_specs=(rows, blocks),
        check_vma=False,
    )
```
